32 devices in a mesh: shard: 4 (over z), group: 8 (over y, x, core).
Axes of the slice: x: 2, y: 2, z: 4, core: 2. Of those that a mesh axis runs over, the one named last changes fastest.
Arguments:
- momentum: bfloat16 [32, 1024, 512], P('group', 'shard'), may hold values from -40 to 40
- gradient: bfloat16 [32, 1024, 512], P('group', 'shard'), may hold values from -300 to 300
- weights: bfloat16 [32, 1024, 512], P('group', 'shard'), may hold values from -0.1875 to 0.1875
- slot_map: int32 [8, 4], P('group'), may hold values from 0 to 1, as said below
- tokens: bfloat16 [4, 8, 256, 1024], P('shard', 'group'), may hold values from -6 to 6
Outputs:
- fresh_state: bfloat16 [32, 1024, 512], P('group', 'shard')
- hidden: bfloat16 [4, 8, 256, 512], P('shard', 'group')
The draws below stay inside these ranges and needn't reach their ends.
Inputs may be any that keep to these rules, and one draw needn't show every extreme that they name: `slot_map`: each row holds every expert-layer of its group at least once and at most four times.
All inputs are finite; a program needn't handle non-finite values.
Results may differ from the reference program's by a relative error of at most 0.014.
Values may be sent and summed in bfloat16 or wider, within the bound.
A program may use at most 64 MiB of HBM per device.

```python
import math
import jax
import jax.numpy as jnp
from jax import lax

D = 1024
F = 512
ITERS = 5
TOK_DEV = 256
OWNERS = 4
GROUPS = 8
MATRICES = 32


def spread_normal(key, salt, level, ramped):
    keys = jax.random.split(jax.random.fold_in(key, salt), 6)
    base = jax.random.normal(keys[0], (MATRICES, D, F), jnp.float32)
    row_scale = jnp.exp(jax.random.uniform(keys[1], (MATRICES, D, 1), jnp.float32) * math.log(10.0))
    column_scale = jnp.exp(jax.random.uniform(keys[2], (MATRICES, 1, F), jnp.float32) * math.log(10.0))
    factor = jnp.ones((MATRICES, D, 1), jnp.float32)
    if ramped:
        row_place = jnp.arange(D, dtype=jnp.float32)[None, :, None] / D
        matrix_place = jnp.arange(MATRICES, dtype=jnp.float32)[:, None, None] / MATRICES
        group_level = jnp.exp(jax.random.uniform(keys[4], (GROUPS,), jnp.float32, -1.0, 1.0))
        block_level = jnp.exp(jax.random.uniform(keys[5], (OWNERS,), jnp.float32, -1.0, 1.0))
        group_factor = jnp.repeat(group_level, MATRICES // GROUPS).reshape(MATRICES, 1, 1)
        block_factor = jnp.repeat(block_level, D // OWNERS).reshape(1, D, 1)
        factor = jnp.sqrt((1.0 + 2.0 * row_place) * (1.0 + matrix_place)) * group_factor * block_factor
    base = jnp.clip(base, -4.0, 4.0)
    return base * row_scale * column_scale * factor * level


def draw_momentum(key, part):
    return spread_normal(key, 11, 0.0465, False).astype(jnp.bfloat16)


def draw_gradient(key, part):
    return jnp.clip(spread_normal(key, 23, 0.1, True), -300.0, 300.0).astype(jnp.bfloat16)


def draw_slot_map(key, part):
    pairs = OWNERS // 2

    def one_group(group_key):
        first_key, second_key = jax.random.split(group_key)
        spare = jnp.repeat(jnp.arange(pairs, dtype=jnp.int32), 3)
        extra = jax.random.permutation(first_key, spare)[:pairs]
        filled = jnp.concatenate([jnp.arange(pairs, dtype=jnp.int32), extra])
        return jax.random.permutation(second_key, filled)
    return jax.vmap(one_group)(jax.random.split(jax.random.fold_in(key, 37), GROUPS))


def steps_of(stream_key, dims, cuts, least, top_value):
    factor_of, own = 1.0, jax.random.fold_in(stream_key, 6)
    for axis_at, shards_of in cuts:
        heights = jnp.exp(jax.random.uniform(jax.random.fold_in(own, axis_at), (shards_of,), jnp.float32, least / len(cuts), top_value / len(cuts)))
        factor_of = factor_of * jnp.repeat(heights, dims[axis_at] // shards_of).reshape([-1 if axis == axis_at else 1 for axis in range(len(dims))])
    return factor_of


def gaussian(key, shape, spread, reach, shards=(), held_as=jnp.bfloat16):
    values = jax.random.normal(key, shape, jnp.float32) * spread
    if len(shards) > 0:
        values = steps_of(key, shape, shards, -0.22, 0.18) * values
    return jnp.clip(values, min=-reach, max=reach).astype(held_as)


def setup_inputs(seed: int = 0) -> dict:
    key_of = jax.random.split(jax.random.key(seed), 6)
    momentum = draw_momentum(jax.random.fold_in(key_of[5], 71), 0)
    gradient = draw_gradient(jax.random.fold_in(key_of[5], 71), 0)
    weights = gaussian(key_of[2], (MATRICES, D, F), D ** -0.5, 0.1875, ((0, 8), (1, 4)))
    slot_map = draw_slot_map(jax.random.fold_in(key_of[5], 71), 0)
    tokens = gaussian(key_of[4], (OWNERS, GROUPS, TOK_DEV, D), 1.0, 6.0, ((0, 4), (1, 8)))
    return dict(momentum=momentum, gradient=gradient, weights=weights, slot_map=slot_map, tokens=tokens)


coefficients = (3.4445, -4.775, 2.0315)
momentum_decay = 0.95
learning_rate = 0.05
clip_rms = 0.5

def orthogonal(matrix):
    widened = matrix.astype(jnp.float32)
    inverse_norm = 1.0 / (jnp.sqrt(jnp.sum(widened * widened)) + 1e-07)
    iterate = (widened * inverse_norm).astype(jnp.bfloat16)
    for iteration in range(ITERS):
        gram = lax.dot_general(iterate, iterate, (((0,), (0,)), ((), ())), preferred_element_type=jnp.float32).astype(jnp.bfloat16)
        squared = jnp.dot(gram, gram, preferred_element_type=jnp.float32)
        polynomial = (coefficients[1] * gram.astype(jnp.float32) + coefficients[2] * squared).astype(jnp.bfloat16)
        product = jnp.dot(iterate, polynomial, preferred_element_type=jnp.float32)
        iterate = (coefficients[0] * iterate.astype(jnp.float32) + product).astype(jnp.bfloat16)
    return (0.2 * math.sqrt(D) * iterate.astype(jnp.float32)).astype(jnp.bfloat16)

def reference(momentum, gradient, weights, slot_map, tokens):
    widened = gradient.astype(jnp.float32)
    grand_total = jnp.sum(widened * widened)
    clip_factor = jnp.minimum(1.0, clip_rms * math.sqrt(MATRICES * D * F) / jnp.sqrt(grand_total + 1e-06))
    fresh_state = (momentum_decay * momentum.astype(jnp.float32) + clip_factor * widened).astype(jnp.bfloat16)
    update = lax.map(orthogonal, fresh_state)
    new_weights = (weights.astype(jnp.float32) - learning_rate * update.astype(jnp.float32)).astype(jnp.bfloat16)
    starts = (jnp.arange(GROUPS, dtype=jnp.int32)[:, None] * OWNERS + 2 * slot_map.astype(jnp.int32)).T.reshape(-1)
    prompts = tokens.reshape(OWNERS * GROUPS, TOK_DEV, D)

    def prefill(item):
        prompt, first = item
        gate_matrix = lax.dynamic_index_in_dim(new_weights, first, 0, keepdims=False)
        up_matrix = lax.dynamic_index_in_dim(new_weights, first + 1, 0, keepdims=False)
        gate_out = jnp.dot(prompt, gate_matrix, preferred_element_type=jnp.float32)
        up_out = jnp.dot(prompt, up_matrix, preferred_element_type=jnp.float32)
        return (jax.nn.silu(gate_out) * up_out).astype(jnp.bfloat16)
    hidden = lax.map(prefill, (prompts, starts)).reshape(OWNERS, GROUPS, TOK_DEV, F)
    return (fresh_state, hidden)
```

```python
import functools
import math

import jax
import jax.numpy as jnp
from jax import lax
from jax.experimental import pallas as pl
from jax.experimental.pallas import tpu as pltpu
from jax.sharding import PartitionSpec as P

ITERS = 5
coefficients = (3.4445, -4.775, 2.0315)
momentum_decay = 0.95
learning_rate = 0.05
clip_rms = 0.5
MESH = pl.DeviceIdType.MESH
f32, bf16 = jnp.float32, jnp.bfloat16


def kernel(
    n, groups, slot_ref, mom_ref, grad_ref, w_ref, tok_ref, fresh_ref, hid_ref,
    part, line_sums, group_sums, x_buf, gram_buf, poly_buf, w_buf, tok_buf, nw_buf, hid_send, hid_recv,
    line_s, line_r, group_s, group_r, x_s, x_r, w_s, w_r, tok_s, tok_r, nw_s, nw_r, hid_s, hid_r,
):
    half = n // 2
    z, g = lax.axis_index("shard"), lax.axis_index("group")
    core = lax.rem(g, 2)
    base = g - core
    side, spot = lax.div(z, half), lax.rem(z, half)
    rows, cols = mom_ref.shape[1], mom_ref.shape[2]
    depth = n * rows
    every_entry = n * groups * depth * cols

    def is_me(zz, gg):
        return jnp.logical_and(zz == z, gg == g)

    def remote(src, dst, ssem, rsem, zz, gg):
        return pltpu.make_async_remote_copy(
            src_ref=src, dst_ref=dst, send_sem=ssem, recv_sem=rsem,
            device_id={"shard": zz, "group": gg}, device_id_type=MESH,
        )

    def ship(src, dst, ssem, rsem, zz, gg):
        same = is_me(zz, gg)

        @pl.when(same)
        def _():
            pltpu.make_async_copy(src, dst, rsem).start()

        @pl.when(jnp.logical_not(same))
        def _():
            remote(src, dst, ssem, rsem, zz, gg).start()

    def sent(src, dst, ssem, rsem, zz, gg):
        @pl.when(jnp.logical_not(is_me(zz, gg)))
        def _():
            remote(src, dst, ssem, rsem, zz, gg).wait_send()

    def landed(dst, rsem):
        pltpu.make_async_copy(dst, dst, rsem).wait()

    barrier = pltpu.get_barrier_semaphore()

    def greet(zz, gg):
        pl.semaphore_signal(barrier, inc=1, device_id={"shard": zz, "group": gg}, device_id_type=MESH)

    for step in range(n):
        greet(lax.rem(z + step, n), base + 1 - core)
        if step:
            greet(lax.rem(z + step, n), g)
    for step in range(2, groups):
        greet(z, lax.rem(base + step, groups))

    def squares(i, total):
        wide = grad_ref[i].astype(f32)
        return total + jnp.sum((wide * wide).reshape(rows // 8, 8, cols), axis=0)

    total = lax.fori_loop(0, n, squares, jnp.zeros((8, cols), f32))
    tile = total[:, :128]
    for at in range(128, cols, 128):
        tile = tile + total[:, at : at + 128]
    part[0] = tile
    pl.semaphore_wait(barrier, 2 * n - 1 + groups - 2)

    for step in range(1, n):
        to = lax.rem(z + step, n)
        remote(part.at[0], line_sums.at[z], line_s.at[step], line_r.at[z], to, g).start()
    line_sums[z] = tile
    for step in range(1, n):
        other = lax.rem(z + step, n)
        landed(line_sums.at[other], line_r.at[other])
    part[1] = jnp.sum(line_sums[...], axis=0)
    for step in range(1, groups):
        to = lax.rem(g + step, groups)
        remote(part.at[1], group_sums.at[g], group_s.at[step], group_r.at[g], z, to).start()
    group_sums[g] = part[1]
    for step in range(1, groups):
        other = lax.rem(g + step, groups)
        landed(group_sums.at[other], group_r.at[other])
    grand_total = jnp.sum(jnp.sum(group_sums[...], axis=0), keepdims=True)
    clip = jnp.minimum(1.0, clip_rms * math.sqrt(every_entry) / jnp.sqrt(grand_total + 1e-06))

    def owner(j):
        return core * half + lax.div(j, 2), base + lax.rem(j, 2)

    my_rows = pl.ds(pl.multiple_of(z * rows, rows), rows)

    def row_copy(j):
        return (fresh_ref.at[j], x_buf.at[my_rows], x_s.at[j], x_r.at[z], *owner(j))

    def weight_copy(j):
        return (w_ref.at[j], w_buf.at[my_rows], w_s.at[j], w_r.at[z], *owner(j))

    slot_core = base + side

    def token_copy(i):
        return (tok_ref.at[0, 0], tok_buf.at[spot], tok_s.at[i], tok_r.at[spot], core * half + i, slot_core)

    def every(count, act):
        def body(i, carry):
            act(i)
            return carry

        lax.fori_loop(0, count, body, 0)

    def freshen(j):
        fresh_ref[j] = (momentum_decay * mom_ref[j].astype(f32) + clip * grad_ref[j].astype(f32)).astype(bf16)
        ship(*row_copy(j))

    every(n, freshen)
    every(n, lambda j: ship(*weight_copy(j)))
    every(half, lambda i: ship(*token_copy(i)))

    def block(d):
        return pl.ds(pl.multiple_of(d * rows, rows), rows)

    every(n, lambda d: landed(x_buf.at[block(d)], x_r.at[d]))

    chunk = 256

    def norm_part(i, acc):
        wide = x_buf[pl.ds(pl.multiple_of(i * chunk, chunk), chunk)].astype(f32)
        return acc + jnp.sum((wide * wide).reshape(chunk // 8, 8, cols), axis=0)

    norm = jnp.sum(lax.fori_loop(0, depth // chunk, norm_part, jnp.zeros((8, cols), f32)), keepdims=True)
    inverse_norm = 1.0 / (jnp.sqrt(norm) + 1e-07)

    def scale(i):
        at = pl.ds(pl.multiple_of(i * chunk, chunk), chunk)
        x_buf[at] = (x_buf[at].astype(f32) * inverse_norm).astype(bf16)

    every(depth // chunk, scale)

    def iterate(_):
        x = x_buf[...]
        gram_buf[...] = lax.dot_general(x, x, (((0,), (0,)), ((), ())), preferred_element_type=f32).astype(bf16)
        gram = gram_buf[...]
        squared = jnp.dot(gram, gram, preferred_element_type=f32)
        poly_buf[...] = (coefficients[1] * gram.astype(f32) + coefficients[2] * squared).astype(bf16)
        x = x_buf[...]
        product = jnp.dot(x, poly_buf[...], preferred_element_type=f32)
        x_buf[...] = (coefficients[0] * x.astype(f32) + product).astype(bf16)

    every(ITERS, iterate)

    every(n, lambda d: landed(w_buf.at[block(d)], w_r.at[d]))

    def renew(i):
        at = pl.ds(pl.multiple_of(i * chunk, chunk), chunk)
        update = (0.2 * math.sqrt(depth) * x_buf[at].astype(f32)).astype(bf16)
        nw_buf[core, at] = (w_buf[at].astype(f32) - learning_rate * update.astype(f32)).astype(bf16)

    every(depth // chunk, renew)
    swap = remote(nw_buf.at[core], nw_buf.at[core], nw_s, nw_r.at[core], z, base + 1 - core)
    swap.start()
    landed(nw_buf.at[1 - core], nw_r.at[1 - core])

    def hidden_copy(i):
        return (hid_send.at[i], hid_recv.at[spot], hid_s.at[i], hid_r.at[spot], core * half + i, base + side)

    def prefill(i):
        landed(tok_buf.at[i], tok_r.at[i])
        prompt = tok_buf[i]
        gate = jnp.dot(prompt, nw_buf[0], preferred_element_type=f32)
        up = jnp.dot(prompt, nw_buf[1], preferred_element_type=f32)
        hid_send[i] = (gate / (1.0 + jnp.exp(-gate)) * up).astype(bf16)
        ship(*hidden_copy(i))

    every(half, prefill)
    every(half, lambda q: landed(hid_recv.at[q], hid_r.at[q]))
    hid_ref[0, 0] = hid_recv[slot_ref[0, z]]

    for step in range(1, n):
        remote(part.at[0], line_sums.at[z], line_s.at[step], line_r.at[z], lax.rem(z + step, n), g).wait_send()
    for step in range(1, groups):
        remote(part.at[1], group_sums.at[g], group_s.at[step], group_r.at[g], z, lax.rem(g + step, groups)).wait_send()
    every(n, lambda j: sent(*row_copy(j)))
    every(n, lambda j: sent(*weight_copy(j)))
    every(half, lambda i: sent(*token_copy(i)))
    every(half, lambda i: sent(*hidden_copy(i)))
    swap.wait_send()


def local(n, groups, momentum, gradient, weights, slot_map, tokens):
    rows, cols = momentum.shape[1:]
    depth, half, prompts = n * rows, n // 2, tokens.shape[2]
    vmem = pl.BlockSpec(memory_space=pltpu.VMEM)
    dma = pltpu.SemaphoreType.DMA
    return pl.pallas_call(
        functools.partial(kernel, n, groups),
        out_shape=(
            jax.ShapeDtypeStruct(momentum.shape, bf16),
            jax.ShapeDtypeStruct((1, 1, prompts, cols), bf16),
        ),
        in_specs=[pl.BlockSpec(memory_space=pltpu.SMEM)] + [vmem] * 4,
        out_specs=(vmem, vmem),
        scratch_shapes=[
            pltpu.VMEM((2, 8, 128), f32),
            pltpu.VMEM((n, 8, 128), f32),
            pltpu.VMEM((groups, 8, 128), f32),
            pltpu.VMEM((depth, cols), bf16),
            pltpu.VMEM((cols, cols), bf16),
            pltpu.VMEM((cols, cols), bf16),
            pltpu.VMEM((depth, cols), bf16),
            pltpu.VMEM((half, prompts, depth), bf16),
            pltpu.VMEM((2, depth, cols), bf16),
            pltpu.VMEM((half, prompts, cols), bf16),
            pltpu.VMEM((half, prompts, cols), bf16),
            dma((n,)), dma((n,)), dma((groups,)), dma((groups,)),
            dma((n,)), dma((n,)), dma((n,)), dma((n,)), dma((half,)), dma((half,)),
            dma(()), dma((2,)), dma((half,)), dma((half,)),
        ],
        compiler_params=pltpu.CompilerParams(
            collective_id=0, has_side_effects=True, vmem_limit_bytes=50 * 2**20
        ),
    )(slot_map, momentum, gradient, weights, tokens)


def solution(mesh):
    in_specs = (
        P("group", "shard", None),
        P("group", "shard", None),
        P("group", "shard", None),
        P("group", None),
        P("shard", "group", None, None),
    )
    out_specs = (P("group", "shard", None), P("shard", "group", None, None))
    step = functools.partial(local, mesh.shape["shard"], mesh.shape["group"])
    return jax.shard_map(step, mesh=mesh, in_specs=in_specs, out_specs=out_specs, check_vma=False)
```

```python
import functools
import math

import jax
import jax.numpy as jnp
from jax import lax
from jax.experimental import pallas as pl
from jax.experimental.pallas import tpu as pltpu
from jax.sharding import PartitionSpec as P

ITERS = 5
coefficients = (3.4445, -4.775, 2.0315)
momentum_decay = 0.95
learning_rate = 0.05
clip_rms = 0.5
MESH = pl.DeviceIdType.MESH
f32, bf16 = jnp.float32, jnp.bfloat16


def kernel(
    n, groups, slot_ref, mom_hbm, grad_hbm, w_ref, tok_ref, fresh_ref, hid_ref,
    mom_ref, grad_ref, part, line_sums, group_sums, x_buf, gram_buf, poly_buf, w_buf, tok_buf, nw_buf, hid_send, hid_recv,
    load_s, line_s, line_r, group_s, group_r, x_s, x_r, w_s, w_r, tok_s, tok_r, pass_s, nw_s, nw_r, hid_s, hid_r,
):
    half = n // 2
    z, g = lax.axis_index("shard"), lax.axis_index("group")
    core = lax.rem(g, 2)
    base = g - core
    side, spot = lax.div(z, half), lax.rem(z, half)
    rows, cols = mom_ref.shape[1], mom_ref.shape[2]
    depth = n * rows
    every_entry = n * groups * depth * cols

    def is_me(zz, gg):
        return jnp.logical_and(zz == z, gg == g)

    def remote(src, dst, ssem, rsem, zz, gg):
        return pltpu.make_async_remote_copy(
            src_ref=src, dst_ref=dst, send_sem=ssem, recv_sem=rsem,
            device_id={"shard": zz, "group": gg}, device_id_type=MESH,
        )

    def ship(src, dst, ssem, rsem, zz, gg):
        same = is_me(zz, gg)

        @pl.when(same)
        def _():
            pltpu.make_async_copy(src, dst, rsem).start()

        @pl.when(jnp.logical_not(same))
        def _():
            remote(src, dst, ssem, rsem, zz, gg).start()

    def sent(src, dst, ssem, rsem, zz, gg):
        @pl.when(jnp.logical_not(is_me(zz, gg)))
        def _():
            remote(src, dst, ssem, rsem, zz, gg).wait_send()

    def landed(dst, rsem):
        pltpu.make_async_copy(dst, dst, rsem).wait()

    load_grad = pltpu.make_async_copy(grad_hbm, grad_ref, load_s.at[0])
    load_mom = pltpu.make_async_copy(mom_hbm, mom_ref, load_s.at[1])
    load_grad.start()
    load_mom.start()

    barrier = pltpu.get_barrier_semaphore()

    def greet(zz, gg):
        pl.semaphore_signal(barrier, inc=1, device_id={"shard": zz, "group": gg}, device_id_type=MESH)

    for step in range(n):
        greet(lax.rem(z + step, n), base + 1 - core)
        if step:
            greet(lax.rem(z + step, n), g)
    for step in range(2, groups):
        greet(z, lax.rem(base + step, groups))

    load_grad.wait()

    def squares(i, total):
        wide = grad_ref[i].astype(f32)
        return total + jnp.sum((wide * wide).reshape(rows // 8, 8, cols), axis=0)

    total = lax.fori_loop(0, n, squares, jnp.zeros((8, cols), f32))
    tile = total[:, :128]
    for at in range(128, cols, 128):
        tile = tile + total[:, at : at + 128]
    part[0] = tile
    pl.semaphore_wait(barrier, 2 * n - 1 + groups - 2)

    for step in range(1, n):
        to = lax.rem(z + step, n)
        remote(part.at[0], line_sums.at[z], line_s.at[step], line_r.at[z], to, g).start()
    line_sums[z] = tile
    for step in range(1, n):
        other = lax.rem(z + step, n)
        landed(line_sums.at[other], line_r.at[other])
    first = core * half
    entry = lax.clamp(first, z, first + half - 1)
    token_copy = (tok_ref.at[0, 0], tok_buf.at[spot], tok_s, tok_r.at[spot], entry, base + side)

    def passing(i, act):
        low = side * half
        enters = lax.clamp(low, core * half + i, low + half - 1)

        @pl.when(jnp.logical_and(z <= enters, z > low))
        def _():
            act(remote(tok_buf.at[i], tok_buf.at[i], pass_s.at[0, i], tok_r.at[i], z - 1, g))

        @pl.when(jnp.logical_and(z >= enters, z < low + half - 1))
        def _():
            act(remote(tok_buf.at[i], tok_buf.at[i], pass_s.at[1, i], tok_r.at[i], z + 1, g))

    ship(*token_copy)
    part[1] = jnp.sum(line_sums[...], axis=0)
    for step in range(1, groups):
        to = lax.rem(g + step, groups)
        remote(part.at[1], group_sums.at[g], group_s.at[step], group_r.at[g], z, to).start()
    group_sums[g] = part[1]
    for step in range(1, groups):
        other = lax.rem(g + step, groups)
        landed(group_sums.at[other], group_r.at[other])
    grand_total = jnp.sum(jnp.sum(group_sums[...], axis=0), keepdims=True)
    clip = jnp.minimum(1.0, clip_rms * math.sqrt(every_entry) / jnp.sqrt(grand_total + 1e-06))

    def owner(j):
        return core * half + lax.div(j, 2), base + lax.rem(j, 2)

    my_rows = pl.ds(pl.multiple_of(z * rows, rows), rows)

    def row_copy(j):
        return (fresh_ref.at[j], x_buf.at[my_rows], x_s.at[j], x_r.at[z], *owner(j))

    def weight_copy(j):
        return (w_ref.at[j], w_buf.at[my_rows], w_s.at[j], w_r.at[z], *owner(j))

    def every(count, act):
        def body(i, carry):
            act(i)
            return carry

        lax.fori_loop(0, count, body, 0)

    def freshen(j):
        fresh_ref[j] = (momentum_decay * mom_ref[j].astype(f32) + clip * grad_ref[j].astype(f32)).astype(bf16)
        ship(*row_copy(j))

    load_mom.wait()
    every(n, freshen)
    every(n, lambda j: ship(*weight_copy(j)))

    def relay(i):
        landed(tok_buf.at[i], tok_r.at[i])
        passing(i, lambda copy: copy.start())

    every(half, relay)

    def block(d):
        return pl.ds(pl.multiple_of(d * rows, rows), rows)

    every(n, lambda d: landed(x_buf.at[block(d)], x_r.at[d]))

    chunk = 256

    def norm_part(i, acc):
        wide = x_buf[pl.ds(pl.multiple_of(i * chunk, chunk), chunk)].astype(f32)
        return acc + jnp.sum((wide * wide).reshape(chunk // 8, 8, cols), axis=0)

    norm = jnp.sum(lax.fori_loop(0, depth // chunk, norm_part, jnp.zeros((8, cols), f32)), keepdims=True)
    inverse_norm = 1.0 / (jnp.sqrt(norm) + 1e-07)

    def scale(i):
        at = pl.ds(pl.multiple_of(i * chunk, chunk), chunk)
        x_buf[at] = (x_buf[at].astype(f32) * inverse_norm).astype(bf16)

    every(depth // chunk, scale)

    def iterate(_):
        x = x_buf[...]
        gram_buf[...] = lax.dot_general(x, x, (((0,), (0,)), ((), ())), preferred_element_type=f32).astype(bf16)
        gram = gram_buf[...]
        squared = jnp.dot(gram, gram, preferred_element_type=f32)
        poly_buf[...] = (coefficients[1] * gram.astype(f32) + coefficients[2] * squared).astype(bf16)
        x = x_buf[...]
        product = jnp.dot(x, poly_buf[...], preferred_element_type=f32)
        x_buf[...] = (coefficients[0] * x.astype(f32) + product).astype(bf16)

    every(ITERS, iterate)

    def swap(d):
        at = block(d)
        return remote(nw_buf.at[core, at], nw_buf.at[core, at], nw_s.at[d], nw_r.at[d], z, base + 1 - core)

    def renew(step):
        d = lax.rem(z + step, n)
        at = block(d)
        update = (0.2 * math.sqrt(depth) * x_buf[at].astype(f32)).astype(bf16)
        landed(w_buf.at[at], w_r.at[d])
        nw_buf[core, at] = (w_buf[at].astype(f32) - learning_rate * update.astype(f32)).astype(bf16)
        swap(d).start()

    every(n, renew)
    every(n, lambda d: landed(nw_buf.at[1 - core, block(d)], nw_r.at[d]))

    def hidden_copy(i):
        return (hid_send.at[i], hid_recv.at[spot], hid_s.at[i], hid_r.at[spot], core * half + i, base + side)

    def prefill(i):
        prompt = tok_buf[i]
        gate = jnp.dot(prompt, nw_buf[0], preferred_element_type=f32)
        up = jnp.dot(prompt, nw_buf[1], preferred_element_type=f32)
        hid_send[i] = (gate / (1.0 + jnp.exp(-gate)) * up).astype(bf16)
        ship(*hidden_copy(i))

    every(half, prefill)
    every(half, lambda q: landed(hid_recv.at[q], hid_r.at[q]))
    hid_ref[0, 0] = hid_recv[slot_ref[0, z]]

    for step in range(1, n):
        remote(part.at[0], line_sums.at[z], line_s.at[step], line_r.at[z], lax.rem(z + step, n), g).wait_send()
    for step in range(1, groups):
        remote(part.at[1], group_sums.at[g], group_s.at[step], group_r.at[g], z, lax.rem(g + step, groups)).wait_send()
    every(n, lambda j: sent(*row_copy(j)))
    every(n, lambda j: sent(*weight_copy(j)))
    sent(*token_copy)
    every(half, lambda i: passing(i, lambda copy: copy.wait_send()))
    every(half, lambda i: sent(*hidden_copy(i)))
    every(n, lambda d: swap(d).wait_send())


def local(n, groups, momentum, gradient, weights, slot_map, tokens):
    rows, cols = momentum.shape[1:]
    depth, half, prompts = n * rows, n // 2, tokens.shape[2]
    vmem = pl.BlockSpec(memory_space=pltpu.VMEM)
    dma = pltpu.SemaphoreType.DMA
    return pl.pallas_call(
        functools.partial(kernel, n, groups),
        out_shape=(
            jax.ShapeDtypeStruct(momentum.shape, bf16),
            jax.ShapeDtypeStruct((1, 1, prompts, cols), bf16),
        ),
        in_specs=[pl.BlockSpec(memory_space=pltpu.SMEM)] + [pl.BlockSpec(memory_space=pl.ANY)] * 4,
        out_specs=(vmem, vmem),
        scratch_shapes=[
            pltpu.VMEM(momentum.shape, bf16),
            pltpu.VMEM(momentum.shape, bf16),
            pltpu.VMEM((2, 8, 128), f32),
            pltpu.VMEM((n, 8, 128), f32),
            pltpu.VMEM((groups, 8, 128), f32),
            pltpu.VMEM((depth, cols), bf16),
            pltpu.VMEM((cols, cols), bf16),
            pltpu.VMEM((cols, cols), bf16),
            pltpu.VMEM((depth, cols), bf16),
            pltpu.VMEM((half, prompts, depth), bf16),
            pltpu.VMEM((2, depth, cols), bf16),
            pltpu.VMEM((half, prompts, cols), bf16),
            pltpu.VMEM((half, prompts, cols), bf16),
            dma((2,)), dma((n,)), dma((n,)), dma((groups,)), dma((groups,)),
            dma((n,)), dma((n,)), dma((n,)), dma((n,)), dma(()), dma((half,)), dma((2, half)),
            dma((n,)), dma((n,)), dma((half,)), dma((half,)),
        ],
        compiler_params=pltpu.CompilerParams(
            collective_id=0, has_side_effects=True, vmem_limit_bytes=62 * 2**20
        ),
    )(slot_map, momentum, gradient, weights, tokens)


def solution(mesh):
    in_specs = (
        P("group", "shard", None),
        P("group", "shard", None),
        P("group", "shard", None),
        P("group", None),
        P("shard", "group", None, None),
    )
    out_specs = (P("group", "shard", None), P("shard", "group", None, None))
    step = functools.partial(local, mesh.shape["shard"], mesh.shape["group"])
    return jax.shard_map(step, mesh=mesh, in_specs=in_specs, out_specs=out_specs, check_vma=False)
```

```python
import functools
import math

import jax
import jax.numpy as jnp
from jax import lax
from jax.experimental import pallas as pl
from jax.experimental.pallas import tpu as pltpu
from jax.sharding import PartitionSpec as P

ITERS = 5
coefficients = (3.4445, -4.775, 2.0315)
momentum_decay = 0.95
learning_rate = 0.05
clip_rms = 0.5
MESH = pl.DeviceIdType.MESH
f32, bf16 = jnp.float32, jnp.bfloat16


def kernel(
    n, groups, slot_ref, mom_hbm, grad_hbm, w_ref, tok_ref, fresh_ref, hid_ref,
    mom_ref, grad_ref, part, line_sums, group_sums, x_buf, gram_buf, poly_buf, w_buf, tok_buf, nw_buf, hid_send, hid_recv,
    load_s, line_s, line_r, group_s, group_r, x_s, x_r, w_s, w_r, tok_s, tok_r, pass_s, nw_s, nw_r, hid_s, hid_r,
):
    half = n // 2
    z, g = lax.axis_index("shard"), lax.axis_index("group")
    core = lax.rem(g, 2)
    base = g - core
    side, spot = lax.div(z, half), lax.rem(z, half)
    rows, cols = mom_ref.shape[1], mom_ref.shape[2]
    depth = n * rows
    every_entry = n * groups * depth * cols

    def is_me(zz, gg):
        return jnp.logical_and(zz == z, gg == g)

    def remote(src, dst, ssem, rsem, zz, gg):
        return pltpu.make_async_remote_copy(
            src_ref=src, dst_ref=dst, send_sem=ssem, recv_sem=rsem,
            device_id={"shard": zz, "group": gg}, device_id_type=MESH,
        )

    def ship(src, dst, ssem, rsem, zz, gg):
        same = is_me(zz, gg)

        @pl.when(same)
        def _():
            pltpu.make_async_copy(src, dst, rsem).start()

        @pl.when(jnp.logical_not(same))
        def _():
            remote(src, dst, ssem, rsem, zz, gg).start()

    def sent(src, dst, ssem, rsem, zz, gg):
        @pl.when(jnp.logical_not(is_me(zz, gg)))
        def _():
            remote(src, dst, ssem, rsem, zz, gg).wait_send()

    def landed(dst, rsem):
        pltpu.make_async_copy(dst, dst, rsem).wait()

    load_grad = pltpu.make_async_copy(grad_hbm, grad_ref, load_s.at[0])
    load_mom = pltpu.make_async_copy(mom_hbm, mom_ref, load_s.at[1])
    load_grad.start()
    load_mom.start()

    barrier = pltpu.get_barrier_semaphore()

    def greet(zz, gg):
        pl.semaphore_signal(barrier, inc=1, device_id={"shard": zz, "group": gg}, device_id_type=MESH)

    for step in range(n):
        greet(lax.rem(z + step, n), base + 1 - core)
        if step:
            greet(lax.rem(z + step, n), g)
    for step in range(2, groups):
        greet(z, lax.rem(base + step, groups))

    load_grad.wait()

    def squares(i, total):
        wide = grad_ref[i].astype(f32)
        return total + jnp.sum((wide * wide).reshape(rows // 8, 8, cols), axis=0)

    total = lax.fori_loop(0, n, squares, jnp.zeros((8, cols), f32))
    tile = total[:, :128]
    for at in range(128, cols, 128):
        tile = tile + total[:, at : at + 128]
    part[0] = tile
    pl.semaphore_wait(barrier, 2 * n - 1 + groups - 2)

    for step in range(1, n):
        to = lax.rem(z + step, n)
        remote(part.at[0], line_sums.at[z], line_s.at[step], line_r.at[z], to, g).start()
    line_sums[z] = tile
    for step in range(1, n):
        other = lax.rem(z + step, n)
        landed(line_sums.at[other], line_r.at[other])
    first = core * half
    entry = lax.clamp(first, z, first + half - 1)
    token_copy = (tok_ref.at[0, 0], tok_buf.at[spot], tok_s, tok_r.at[spot], entry, base + side)

    def passing(i, act):
        low = side * half
        enters = lax.clamp(low, core * half + i, low + half - 1)

        @pl.when(jnp.logical_and(z <= enters, z > low))
        def _():
            act(remote(tok_buf.at[i], tok_buf.at[i], pass_s.at[0, i], tok_r.at[i], z - 1, g))

        @pl.when(jnp.logical_and(z >= enters, z < low + half - 1))
        def _():
            act(remote(tok_buf.at[i], tok_buf.at[i], pass_s.at[1, i], tok_r.at[i], z + 1, g))

    ship(*token_copy)
    part[1] = jnp.sum(line_sums[...], axis=0)
    for step in range(1, groups):
        to = lax.rem(g + step, groups)
        remote(part.at[1], group_sums.at[g], group_s.at[step], group_r.at[g], z, to).start()
    group_sums[g] = part[1]
    for step in range(1, groups):
        other = lax.rem(g + step, groups)
        landed(group_sums.at[other], group_r.at[other])
    grand_total = jnp.sum(jnp.sum(group_sums[...], axis=0), keepdims=True)
    clip = jnp.minimum(1.0, clip_rms * math.sqrt(every_entry) / jnp.sqrt(grand_total + 1e-06))

    def owner(j):
        return core * half + lax.div(j, 2), base + lax.rem(j, 2)

    my_rows = pl.ds(pl.multiple_of(z * rows, rows), rows)

    def row_copy(j):
        return (fresh_ref.at[j], x_buf.at[my_rows], x_s.at[j], x_r.at[z], *owner(j))

    def weight_copy(j):
        return (w_ref.at[j], w_buf.at[my_rows], w_s.at[j], w_r.at[z], *owner(j))

    def every(count, act):
        def body(i, carry):
            act(i)
            return carry

        lax.fori_loop(0, count, body, 0)

    def freshen(j):
        fresh_ref[j] = (momentum_decay * mom_ref[j].astype(f32) + clip * grad_ref[j].astype(f32)).astype(bf16)
        ship(*row_copy(j))

    load_mom.wait()
    every(n, freshen)
    every(half, lambda j: ship(*weight_copy(2 * j)))

    def relay(i):
        landed(tok_buf.at[i], tok_r.at[i])
        passing(i, lambda copy: copy.start())

    every(half, relay)

    def block(d):
        return pl.ds(pl.multiple_of(d * rows, rows), rows)

    every(n, lambda d: landed(x_buf.at[block(d)], x_r.at[d]))
    every(half, lambda j: ship(*weight_copy(2 * j + 1)))

    chunk = 256

    def norm_part(i, acc):
        wide = x_buf[pl.ds(pl.multiple_of(i * chunk, chunk), chunk)].astype(f32)
        return acc + jnp.sum((wide * wide).reshape(chunk // 8, 8, cols), axis=0)

    norm = jnp.sum(lax.fori_loop(0, depth // chunk, norm_part, jnp.zeros((8, cols), f32)), keepdims=True)
    inverse_norm = 1.0 / (jnp.sqrt(norm) + 1e-07)

    def scale(i):
        at = pl.ds(pl.multiple_of(i * chunk, chunk), chunk)
        x_buf[at] = (x_buf[at].astype(f32) * inverse_norm).astype(bf16)

    every(depth // chunk, scale)

    def iterate(_):
        x = x_buf[...]
        gram_buf[...] = lax.dot_general(x, x, (((0,), (0,)), ((), ())), preferred_element_type=f32).astype(bf16)
        gram = gram_buf[...]
        squared = jnp.dot(gram, gram, preferred_element_type=f32)
        poly_buf[...] = (coefficients[1] * gram.astype(f32) + coefficients[2] * squared).astype(bf16)
        x = x_buf[...]
        product = jnp.dot(x, poly_buf[...], preferred_element_type=f32)
        x_buf[...] = (coefficients[0] * x.astype(f32) + product).astype(bf16)

    every(ITERS, iterate)

    def swap(d):
        at = block(d)
        return remote(nw_buf.at[core, at], nw_buf.at[core, at], nw_s.at[d], nw_r.at[d], z, base + 1 - core)

    def renew(step):
        d = lax.rem(z + step, n)
        at = block(d)
        update = (0.2 * math.sqrt(depth) * x_buf[at].astype(f32)).astype(bf16)
        landed(w_buf.at[at], w_r.at[d])
        nw_buf[core, at] = (w_buf[at].astype(f32) - learning_rate * update.astype(f32)).astype(bf16)
        swap(d).start()

    every(n, renew)
    every(n, lambda d: landed(nw_buf.at[1 - core, block(d)], nw_r.at[d]))

    def hidden_copy(i):
        return (hid_send.at[i], hid_recv.at[spot], hid_s.at[i], hid_r.at[spot], core * half + i, base + side)

    def prefill(i):
        prompt = tok_buf[i]
        gate = jnp.dot(prompt, nw_buf[0], preferred_element_type=f32)
        up = jnp.dot(prompt, nw_buf[1], preferred_element_type=f32)
        hid_send[i] = (gate / (1.0 + jnp.exp(-gate)) * up).astype(bf16)
        ship(*hidden_copy(i))

    every(half, prefill)
    every(half, lambda q: landed(hid_recv.at[q], hid_r.at[q]))
    hid_ref[0, 0] = hid_recv[slot_ref[0, z]]

    for step in range(1, n):
        remote(part.at[0], line_sums.at[z], line_s.at[step], line_r.at[z], lax.rem(z + step, n), g).wait_send()
    for step in range(1, groups):
        remote(part.at[1], group_sums.at[g], group_s.at[step], group_r.at[g], z, lax.rem(g + step, groups)).wait_send()
    every(n, lambda j: sent(*row_copy(j)))
    every(n, lambda j: sent(*weight_copy(j)))
    sent(*token_copy)
    every(half, lambda i: passing(i, lambda copy: copy.wait_send()))
    every(half, lambda i: sent(*hidden_copy(i)))
    every(n, lambda d: swap(d).wait_send())


def local(n, groups, momentum, gradient, weights, slot_map, tokens):
    rows, cols = momentum.shape[1:]
    depth, half, prompts = n * rows, n // 2, tokens.shape[2]
    vmem = pl.BlockSpec(memory_space=pltpu.VMEM)
    dma = pltpu.SemaphoreType.DMA
    return pl.pallas_call(
        functools.partial(kernel, n, groups),
        out_shape=(
            jax.ShapeDtypeStruct(momentum.shape, bf16),
            jax.ShapeDtypeStruct((1, 1, prompts, cols), bf16),
        ),
        in_specs=[pl.BlockSpec(memory_space=pltpu.SMEM)] + [pl.BlockSpec(memory_space=pl.ANY)] * 4,
        out_specs=(vmem, vmem),
        scratch_shapes=[
            pltpu.VMEM(momentum.shape, bf16),
            pltpu.VMEM(momentum.shape, bf16),
            pltpu.VMEM((2, 8, 128), f32),
            pltpu.VMEM((n, 8, 128), f32),
            pltpu.VMEM((groups, 8, 128), f32),
            pltpu.VMEM((depth, cols), bf16),
            pltpu.VMEM((cols, cols), bf16),
            pltpu.VMEM((cols, cols), bf16),
            pltpu.VMEM((depth, cols), bf16),
            pltpu.VMEM((half, prompts, depth), bf16),
            pltpu.VMEM((2, depth, cols), bf16),
            pltpu.VMEM((half, prompts, cols), bf16),
            pltpu.VMEM((half, prompts, cols), bf16),
            dma((2,)), dma((n,)), dma((n,)), dma((groups,)), dma((groups,)),
            dma((n,)), dma((n,)), dma((n,)), dma((n,)), dma(()), dma((half,)), dma((2, half)),
            dma((n,)), dma((n,)), dma((half,)), dma((half,)),
        ],
        compiler_params=pltpu.CompilerParams(
            collective_id=0, has_side_effects=True, vmem_limit_bytes=62 * 2**20
        ),
    )(slot_map, momentum, gradient, weights, tokens)


def solution(mesh):
    in_specs = (
        P("group", "shard", None),
        P("group", "shard", None),
        P("group", "shard", None),
        P("group", None),
        P("shard", "group", None, None),
    )
    out_specs = (P("group", "shard", None), P("shard", "group", None, None))
    step = functools.partial(local, mesh.shape["shard"], mesh.shape["group"])
    return jax.shard_map(step, mesh=mesh, in_specs=in_specs, out_specs=out_specs, check_vma=False)
```

```python
import functools
import math

import jax
import jax.numpy as jnp
from jax import lax
from jax.experimental import pallas as pl
from jax.experimental.pallas import tpu as pltpu
from jax.sharding import PartitionSpec as P

ITERS = 5
coefficients = (3.4445, -4.775, 2.0315)
momentum_decay = 0.95
learning_rate = 0.05
clip_rms = 0.5
MESH = pl.DeviceIdType.MESH
f32, bf16 = jnp.float32, jnp.bfloat16


def kernel(
    n, groups, slot_ref, mom_hbm, grad_hbm, w_ref, tok_ref, fresh_ref, hid_ref,
    mom_ref, grad_ref, part, line_sums, group_sums, x_buf, gram_buf, poly_buf, w_buf, tok_buf, nw_buf, hid_send, hid_recv,
    load_s, line_s, line_r, group_s, group_r, x_s, x_r, w_s, w_r, tok_s, tok_r, pass_s, nw_s, nw_r, hid_s, hid_r,
):
    half = n // 2
    z, g = lax.axis_index("shard"), lax.axis_index("group")
    core = lax.rem(g, 2)
    base = g - core
    side, spot = lax.div(z, half), lax.rem(z, half)
    rows, cols = mom_ref.shape[1], mom_ref.shape[2]
    depth = n * rows
    every_entry = n * groups * depth * cols

    def is_me(zz, gg):
        return jnp.logical_and(zz == z, gg == g)

    def remote(src, dst, ssem, rsem, zz, gg):
        return pltpu.make_async_remote_copy(
            src_ref=src, dst_ref=dst, send_sem=ssem, recv_sem=rsem,
            device_id={"shard": zz, "group": gg}, device_id_type=MESH,
        )

    def ship(src, dst, ssem, rsem, zz, gg):
        same = is_me(zz, gg)

        @pl.when(same)
        def _():
            pltpu.make_async_copy(src, dst, rsem).start()

        @pl.when(jnp.logical_not(same))
        def _():
            remote(src, dst, ssem, rsem, zz, gg).start()

    def sent(src, dst, ssem, rsem, zz, gg):
        @pl.when(jnp.logical_not(is_me(zz, gg)))
        def _():
            remote(src, dst, ssem, rsem, zz, gg).wait_send()

    def landed(dst, rsem):
        pltpu.make_async_copy(dst, dst, rsem).wait()

    load_grad = pltpu.make_async_copy(grad_hbm, grad_ref, load_s.at[0])
    load_mom = pltpu.make_async_copy(mom_hbm, mom_ref, load_s.at[1])
    load_grad.start()
    load_mom.start()

    barrier = pltpu.get_barrier_semaphore()

    def greet(zz, gg):
        pl.semaphore_signal(barrier, inc=1, device_id={"shard": zz, "group": gg}, device_id_type=MESH)

    for step in range(n):
        greet(lax.rem(z + step, n), base + 1 - core)
        if step:
            greet(lax.rem(z + step, n), g)
    for step in range(2, groups):
        greet(z, lax.rem(base + step, groups))

    load_grad.wait()

    def squares(i, total):
        wide = grad_ref[i].astype(f32)
        return total + jnp.sum((wide * wide).reshape(rows // 8, 8, cols), axis=0)

    total = lax.fori_loop(0, n, squares, jnp.zeros((8, cols), f32))
    tile = total[:, :128]
    for at in range(128, cols, 128):
        tile = tile + total[:, at : at + 128]
    part[0] = tile
    pl.semaphore_wait(barrier, 2 * n - 1 + groups - 2)

    for step in range(1, n):
        to = lax.rem(z + step, n)
        remote(part.at[0], line_sums.at[z], line_s.at[step], line_r.at[z], to, g).start()
    line_sums[z] = tile
    for step in range(1, n):
        other = lax.rem(z + step, n)
        landed(line_sums.at[other], line_r.at[other])
    first = core * half
    entry = lax.clamp(first, z, first + half - 1)
    token_copy = (tok_ref.at[0, 0], tok_buf.at[spot], tok_s, tok_r.at[spot], entry, base + side)

    def passing(i, act):
        low = side * half
        enters = lax.clamp(low, core * half + i, low + half - 1)

        @pl.when(jnp.logical_and(z <= enters, z > low))
        def _():
            act(remote(tok_buf.at[i], tok_buf.at[i], pass_s.at[0, i], tok_r.at[i], z - 1, g))

        @pl.when(jnp.logical_and(z >= enters, z < low + half - 1))
        def _():
            act(remote(tok_buf.at[i], tok_buf.at[i], pass_s.at[1, i], tok_r.at[i], z + 1, g))

    ship(*token_copy)
    part[1] = jnp.sum(line_sums[...], axis=0)
    for step in range(1, groups):
        to = lax.rem(g + step, groups)
        remote(part.at[1], group_sums.at[g], group_s.at[step], group_r.at[g], z, to).start()
    group_sums[g] = part[1]
    for step in range(1, groups):
        other = lax.rem(g + step, groups)
        landed(group_sums.at[other], group_r.at[other])
    grand_total = jnp.sum(jnp.sum(group_sums[...], axis=0), keepdims=True)
    clip = jnp.minimum(1.0, clip_rms * math.sqrt(every_entry) / jnp.sqrt(grand_total + 1e-06))

    def owner(j):
        return core * half + lax.div(j, 2), base + lax.rem(j, 2)

    my_rows = pl.ds(pl.multiple_of(z * rows, rows), rows)

    def row_copy(j):
        return (fresh_ref.at[j], x_buf.at[my_rows], x_s.at[j], x_r.at[z], *owner(j))

    def weight_copy(j):
        return (w_ref.at[j], w_buf.at[my_rows], w_s.at[j], w_r.at[z], *owner(j))

    def every(count, act):
        def body(i, carry):
            act(i)
            return carry

        lax.fori_loop(0, count, body, 0)

    def freshen(j):
        fresh_ref[j] = (momentum_decay * mom_ref[j].astype(f32) + clip * grad_ref[j].astype(f32)).astype(bf16)
        ship(*row_copy(j))

    load_mom.wait()
    every(n, freshen)
    every(half, lambda j: ship(*weight_copy(2 * j + 1)))

    def relay(i):
        landed(tok_buf.at[i], tok_r.at[i])
        passing(i, lambda copy: copy.start())

    every(half, relay)

    def block(d):
        return pl.ds(pl.multiple_of(d * rows, rows), rows)

    every(n, lambda d: landed(x_buf.at[block(d)], x_r.at[d]))
    every(half, lambda j: ship(*weight_copy(2 * j)))

    chunk = 256

    def norm_part(i, acc):
        wide = x_buf[pl.ds(pl.multiple_of(i * chunk, chunk), chunk)].astype(f32)
        return acc + jnp.sum((wide * wide).reshape(chunk // 8, 8, cols), axis=0)

    norm = jnp.sum(lax.fori_loop(0, depth // chunk, norm_part, jnp.zeros((8, cols), f32)), keepdims=True)
    inverse_norm = 1.0 / (jnp.sqrt(norm) + 1e-07)

    def scale(i):
        at = pl.ds(pl.multiple_of(i * chunk, chunk), chunk)
        x_buf[at] = (x_buf[at].astype(f32) * inverse_norm).astype(bf16)

    every(depth // chunk, scale)

    def iterate(_):
        x = x_buf[...]
        gram_buf[...] = lax.dot_general(x, x, (((0,), (0,)), ((), ())), preferred_element_type=f32).astype(bf16)
        gram = gram_buf[...]
        squared = jnp.dot(gram, gram, preferred_element_type=f32)
        poly_buf[...] = (coefficients[1] * gram.astype(f32) + coefficients[2] * squared).astype(bf16)
        x = x_buf[...]
        product = jnp.dot(x, poly_buf[...], preferred_element_type=f32)
        x_buf[...] = (coefficients[0] * x.astype(f32) + product).astype(bf16)

    every(ITERS, iterate)

    def swap(d):
        at = block(d)
        return remote(nw_buf.at[core, at], nw_buf.at[core, at], nw_s.at[d], nw_r.at[d], z, base + 1 - core)

    def renew(step):
        d = lax.rem(z + step, n)
        at = block(d)
        update = (0.2 * math.sqrt(depth) * x_buf[at].astype(f32)).astype(bf16)
        landed(w_buf.at[at], w_r.at[d])
        nw_buf[core, at] = (w_buf[at].astype(f32) - learning_rate * update.astype(f32)).astype(bf16)
        swap(d).start()

    every(n, renew)
    every(n, lambda d: landed(nw_buf.at[1 - core, block(d)], nw_r.at[d]))

    def hidden_copy(i):
        return (hid_send.at[i], hid_recv.at[spot], hid_s.at[i], hid_r.at[spot], core * half + i, base + side)

    def prefill(i):
        prompt = tok_buf[i]
        gate = jnp.dot(prompt, nw_buf[0], preferred_element_type=f32)
        up = jnp.dot(prompt, nw_buf[1], preferred_element_type=f32)
        hid_send[i] = (gate / (1.0 + jnp.exp(-gate)) * up).astype(bf16)
        ship(*hidden_copy(i))

    every(half, prefill)
    every(half, lambda q: landed(hid_recv.at[q], hid_r.at[q]))
    hid_ref[0, 0] = hid_recv[slot_ref[0, z]]

    for step in range(1, n):
        remote(part.at[0], line_sums.at[z], line_s.at[step], line_r.at[z], lax.rem(z + step, n), g).wait_send()
    for step in range(1, groups):
        remote(part.at[1], group_sums.at[g], group_s.at[step], group_r.at[g], z, lax.rem(g + step, groups)).wait_send()
    every(n, lambda j: sent(*row_copy(j)))
    every(n, lambda j: sent(*weight_copy(j)))
    sent(*token_copy)
    every(half, lambda i: passing(i, lambda copy: copy.wait_send()))
    every(half, lambda i: sent(*hidden_copy(i)))
    every(n, lambda d: swap(d).wait_send())


def local(n, groups, momentum, gradient, weights, slot_map, tokens):
    rows, cols = momentum.shape[1:]
    depth, half, prompts = n * rows, n // 2, tokens.shape[2]
    vmem = pl.BlockSpec(memory_space=pltpu.VMEM)
    dma = pltpu.SemaphoreType.DMA
    return pl.pallas_call(
        functools.partial(kernel, n, groups),
        out_shape=(
            jax.ShapeDtypeStruct(momentum.shape, bf16),
            jax.ShapeDtypeStruct((1, 1, prompts, cols), bf16),
        ),
        in_specs=[pl.BlockSpec(memory_space=pltpu.SMEM)] + [pl.BlockSpec(memory_space=pl.ANY)] * 4,
        out_specs=(vmem, vmem),
        scratch_shapes=[
            pltpu.VMEM(momentum.shape, bf16),
            pltpu.VMEM(momentum.shape, bf16),
            pltpu.VMEM((2, 8, 128), f32),
            pltpu.VMEM((n, 8, 128), f32),
            pltpu.VMEM((groups, 8, 128), f32),
            pltpu.VMEM((depth, cols), bf16),
            pltpu.VMEM((cols, cols), bf16),
            pltpu.VMEM((cols, cols), bf16),
            pltpu.VMEM((depth, cols), bf16),
            pltpu.VMEM((half, prompts, depth), bf16),
            pltpu.VMEM((2, depth, cols), bf16),
            pltpu.VMEM((half, prompts, cols), bf16),
            pltpu.VMEM((half, prompts, cols), bf16),
            dma((2,)), dma((n,)), dma((n,)), dma((groups,)), dma((groups,)),
            dma((n,)), dma((n,)), dma((n,)), dma((n,)), dma(()), dma((half,)), dma((2, half)),
            dma((n,)), dma((n,)), dma((half,)), dma((half,)),
        ],
        compiler_params=pltpu.CompilerParams(
            collective_id=0, has_side_effects=True, vmem_limit_bytes=62 * 2**20
        ),
    )(slot_map, momentum, gradient, weights, tokens)


def solution(mesh):
    in_specs = (
        P("group", "shard", None),
        P("group", "shard", None),
        P("group", "shard", None),
        P("group", None),
        P("shard", "group", None, None),
    )
    out_specs = (P("group", "shard", None), P("shard", "group", None, None))
    step = functools.partial(local, mesh.shape["shard"], mesh.shape["group"])
    return jax.shard_map(step, mesh=mesh, in_specs=in_specs, out_specs=out_specs, check_vma=False)
```
